128 devices in a mesh: row: 16 (over y_lo, x, core), col: 8 (over z, y_hi).
Axes of the slice: x: 4, y: 4 (y_hi: 2, y_lo: 2; y = y_hi * 2 + y_lo), z: 4, core: 2. Of those that a mesh axis runs over, the one named last changes fastest.
Arguments:
- x_blocks: float32 [256, 32, 4096], P('row', 'col'), may hold values from -1 to 1, as said below
- block_cols: int32 [256, 32], P('row', 'col'), may hold values from -1 to 255, as said below
Outputs:
- square: float32 [256, 32, 4096], P('row', 'col')
- updated: float32 [256, 32, 4096], P('row', 'col')
The draws below stay inside these ranges and needn't reach their ends.
Inputs may be any that keep to these rules, and one draw needn't show every extreme that they name: `block_cols`: slots (c * 4) to (c * 4 + 3) of a block row hold distinct block columns of group c, that is columns c * 256 // 8 to (c + 1) * 256 // 8 - 1, in increasing order, with the empty slots (-1) last. Every block row holds its own column, holds at most 15 columns, and the pattern is symmetric: row i holds column j exactly when row j holds column i. `x_blocks`: the matrix is symmetric: the block of row j at the slot of column i is the transpose of the block of row i at the slot of column j. Its spectral norm is below one. Empty slots hold zeros.
All inputs are finite; a program needn't handle non-finite values.
Results may differ from the reference program's by a relative error of at most 0.0003.
Values sent between devices are 32-bit elements; how exact they have to be, the bound alone decides.
A program may use at most 128 MiB of HBM per device.

```python
import jax
import jax.numpy as jnp
from jax import lax

BS = 64
KC = 4
BAND = 7
RB = 16
N_ROW = 16
N_COL = 8


noise_scale = 0.007


diagonal_reach = 0.5


def shared_pattern(key):
    every = RB * N_ROW
    group = every // N_COL
    places = jax.random.permutation(key, every).astype(jnp.int32)
    spacing = jnp.abs(places[:, None] - places[None, :])
    spacing = jnp.minimum(spacing, every - spacing)
    indices = jnp.arange(every, dtype=jnp.int32)
    itself = indices[:, None] == indices[None, :]
    others = (spacing <= BAND) & jnp.logical_not(itself)
    grouped = others.reshape(every, N_COL, group)
    ranking = jnp.cumsum(grouped.astype(jnp.int32), axis=2)
    keep = (grouped & (ranking <= KC - 1)).reshape(every, every)
    return keep & keep.T | itself


def slot_columns(keep):
    every = RB * N_ROW
    group = every // N_COL
    grouped = keep.reshape(every, N_COL, group)
    ranking = jnp.cumsum(grouped.astype(jnp.int32), axis=2)
    numbers = jnp.arange(1, KC + 1, dtype=jnp.int32)
    picked = grouped[:, :, :, None] & (ranking[:, :, :, None] == numbers[None, None, None, :])
    within = jnp.sum(picked.astype(jnp.int32) * jnp.arange(group, dtype=jnp.int32)[None, None, :, None], axis=2)
    found = jnp.any(picked, axis=2)
    offsets = jnp.arange(N_COL, dtype=jnp.int32)[None, :, None] * group
    columns = jnp.where(found, within + offsets, -1)
    return columns.reshape(every, N_COL * KC).astype(jnp.int32)


def draw_block_cols(key, part):
    keep = shared_pattern(key)
    return slot_columns(keep)


def draw_x_blocks(key, part):
    keep = shared_pattern(key)
    key = jax.random.fold_in(key, 23)
    every = RB * N_ROW
    slots = N_COL * KC
    columns = slot_columns(keep)
    rows_here = jnp.broadcast_to(jnp.arange(every, dtype=jnp.int32)[:, None], (every, slots))
    cols_here = jnp.maximum(columns, 0)
    lower = jnp.minimum(rows_here, cols_here)
    upper = jnp.maximum(rows_here, cols_here)
    pair = (lower * every + upper).reshape(-1)
    noise_key = jax.random.fold_in(key, 1)

    def one_block(number):
        return jax.random.normal(jax.random.fold_in(noise_key, number), (BS, BS), jnp.float32)
    blocks = jax.vmap(one_block)(pair).reshape(every, slots, BS, BS)
    swapped = jnp.swapaxes(blocks, 2, 3)
    flip = (rows_here > cols_here)[:, :, None, None]
    same = (rows_here == cols_here)[:, :, None, None]
    blocks = jnp.where(flip, swapped, blocks)
    blocks = jnp.where(same, 0.5 * (blocks + swapped), blocks)
    shifts = jax.random.uniform(jax.random.fold_in(key, 2), (every, BS), jnp.float32, -diagonal_reach, diagonal_reach)
    unit = jnp.eye(BS, dtype=jnp.float32)
    diagonal_part = unit[None, None, :, :] * shifts[:, None, None, :]
    blocks = noise_scale * blocks + jnp.where(same, diagonal_part, 0.0)
    blocks = jnp.where((columns >= 0)[:, :, None, None], blocks, 0.0)
    return blocks.reshape(every, slots, BS * BS).astype(jnp.float32)


def setup_inputs(seed: int = 0) -> dict:
    keys = jax.random.split(jax.random.key(seed), 3)
    x_blocks = draw_x_blocks(jax.random.fold_in(keys[2], 71), 0)
    block_cols = draw_block_cols(jax.random.fold_in(keys[2], 71), 0)
    return {"x_blocks": x_blocks, "block_cols": block_cols}


def tile_product(left, right, block_cols):
    slot_count = N_COL * KC
    is_used = block_cols >= 0

    def one_row(packed):
        left_vals, left_cols, left_used = packed
        right_rows = jnp.where(left_used, left_cols, 0).astype(jnp.int32)
        right_vals = right[right_rows]
        right_cols = block_cols[right_rows]
        matches = (right_cols[:, None, :] == left_cols[None, :, None]) & left_used[None, :, None] & left_used[:, None, None]
        where_u = jnp.sum(matches.astype(jnp.int32) * jnp.arange(slot_count, dtype=jnp.int32)[None, None, :], axis=2)
        present = jnp.any(matches, axis=2)
        chosen = jnp.take_along_axis(right_vals, where_u[:, :, None], axis=1)
        chosen = jnp.where(present[:, :, None], chosen, jnp.zeros_like(chosen))
        result = jnp.einsum("tab,tsbc->sac", left_vals.reshape(slot_count, BS, BS), chosen.reshape(slot_count, slot_count, BS, BS), precision=lax.Precision.HIGHEST)
        return result.reshape(slot_count, BS * BS)

    return lax.map(one_row, (left, block_cols, is_used))


def reference(x_blocks, block_cols):
    cleaned = jnp.where((block_cols >= 0)[:, :, None], x_blocks, jnp.zeros_like(x_blocks))
    square = tile_product(cleaned, cleaned, block_cols)
    updated = 1.5 * cleaned - 0.5 * tile_product(cleaned, square, block_cols)
    return square, updated
```

```python
import heapq

import jax
import jax.numpy as jnp
from jax import lax
from jax.experimental import pallas as pl
from jax.experimental.pallas import tpu as pltpu
from jax.sharding import PartitionSpec as P

MESH = pl.DeviceIdType.MESH

ROWS = 16
KC = 4
N_R = 16
N_C = 8
PIECES = 8
STEP = ROWS // PIECES
PIECE_US = 23.0 / PIECES
HOP_US = 1.5
COLS = PIECES

OWN = (0, 0)
MESSAGES = [(d, p) for d in range(4) for p in range(2)]


def slot(message):
    return message[0] * 2 + message[1]


def tree(piece, pair_first):
    def route(message):
        d, p = message
        if d == 2:
            forward = (piece + (p if pair_first else 0)) % 2 == 0
            ring = ["+", "+"] if forward else ["-", "-"]
        else:
            ring = [[], ["+"], None, ["-"]][d]
        pair = ["pair"] * p
        return tuple(pair + ring if pair_first else ring + pair)

    by_route = {route(m): m for m in MESSAGES}
    children = {m: [] for m in MESSAGES}
    for m in MESSAGES:
        if m != OWN:
            r = route(m)
            children[by_route[r[:-1]]].append((r[-1], m))
    return children


def plan(gathers):
    free = {}
    order = []
    queue = []
    count = 0
    for name, trees, links in gathers:
        for piece in [COLS] + list(range(PIECES)):
            count += 1
            heapq.heappush(queue, (0.01 * (piece + 1) if piece != COLS else 0.0, count, name, OWN, piece))
    table = {name: (trees, links) for name, trees, links in gathers}
    while queue:
        now, _, name, message, piece = heapq.heappop(queue)
        if message != OWN:
            order.append((now, name, message, piece))
        trees, links = table[name]
        for link, child in trees[piece][message]:
            wire = links[link]
            start = max(now, free.get(wire, 0.0))
            free[wire] = start + (0.05 if piece == COLS else PIECE_US)
            count += 1
            heapq.heappush(queue, (free[wire] + HOP_US, count, name, child, piece))
    return sorted(order, key=lambda e: e[0])


def trees_of(pair_first):
    return [tree(k, pair_first[k]) for k in range(PIECES)] + [tree(0, True)]


R_TREES = trees_of([k % 4 != 3 for k in range(PIECES)])
L_TREES = trees_of([True] * PIECES)
S_TREES = trees_of([k % 8 not in (2, 5, 7) for k in range(PIECES)])
R_LINKS = {"+": "x+", "-": "x-", "pair": "y"}
L_LINKS = {"+": "z+", "-": "z-", "pair": "y"}


class Place:
    def __init__(self):
        self.r = lax.axis_index("row")
        self.c = lax.axis_index("col")
        self.core = self.r % 2
        self.x = (self.r // 2) % 4
        self.yl = self.r // 8
        self.z = self.c // 2
        self.yh = self.c % 2
        self.q = self.r // 2

    def row_of(self, x, yl, core):
        return (yl * 4 + x) * 2 + core

    def row_source(self, message):
        d, p = message
        yl = 1 - self.yl if p else self.yl
        return self.row_of((self.x + 4 - d) % 4, yl, self.core)

    def col_source(self, message):
        d, p = message
        yh = 1 - self.yh if p else self.yh
        return ((self.z + 4 - d) % 4) * 2 + yh

    def row_neighbour(self, link):
        if link == "pair":
            return (self.row_of(self.x, 1 - self.yl, self.core), self.c)
        return (self.row_of((self.x + (1 if link == "+" else 3)) % 4, self.yl, self.core), self.c)

    def col_neighbour(self, link):
        if link == "pair":
            return (self.r, self.z * 2 + 1 - self.yh)
        return (self.r, ((self.z + (1 if link == "+" else 3)) % 4) * 2 + self.yh)

    def sibling(self):
        return (self.row_of(self.x, self.yl, 1 - self.core), self.c)


def remote(ref, send, recv, device, to=None):
    return pltpu.make_async_remote_copy(
        src_ref=ref,
        dst_ref=ref if to is None else to,
        send_sem=send,
        recv_sem=recv,
        device_id=device,
        device_id_type=MESH,
    )


def kernel(
    x_ref, tile_ref, cs_ref, sq_ref, up_ref,
    rp, lp, acc, pc, lc, pc_s, lc_s,
    send, cols_send, r_recv, l_recv, s_recv, r_sib, s_sib, pair_sem, local_sem,
    *sp,
):
    place = Place()
    r, c, q = place.r, place.c, place.q
    sibling = place.sibling()
    lane = lax.broadcasted_iota(jnp.int32, (64, 128), 1)
    lane_half = lax.broadcasted_iota(jnp.int32, (32, 128), 1) < 64

    barrier = pltpu.get_barrier_semaphore()
    neighbours = [place.row_neighbour(k) for k in ("+", "-", "pair")]
    neighbours += [place.col_neighbour(k) for k in ("+", "-", "pair")] + [sibling]
    for device in neighbours:
        pl.semaphore_signal(barrier, inc=1, device_id=device, device_id_type=MESH)

    def convert(i, carry):
        for h in range(2):
            pair = []
            for u in (2 * h, 2 * h + 1):
                v = x_ref[i, pl.ds(u, 32, stride=4), :]
                pair.append(jnp.where(cs_ref[i * KC + u] >= 0, v, 0.0))
            even = jnp.where(lane_half, pair[0], pltpu.roll(pair[1], 64, 1))
            odd = jnp.where(lane_half, pltpu.roll(pair[0], 64, 1), pair[1])
            for panel, n in ((rp, r), (lp, c)):
                panel[n, i, h, pl.ds(0, 32, stride=2), :] = even
                panel[n, i, h, pl.ds(1, 32, stride=2), :] = odd
        return carry

    lax.fori_loop(0, ROWS, convert, 0)
    pc[q, place.core] = tile_ref[...]
    lc[c] = tile_ref[...]
    pl.semaphore_wait(barrier, len(neighbours))

    def ref_of(name, message, piece):
        if name == "L":
            n = place.col_source(message)
            return lc.at[n] if piece == COLS else lp.at[n, pl.ds(piece * STEP, STEP)]
        if name == "S":
            return sp[slot(message)].at[place.core, pl.ds(piece * STEP, STEP)]
        n = place.row_source(message)
        return pc.at[n // 2] if piece == COLS else rp.at[n, pl.ds(piece * STEP, STEP)]

    trees = {"R": R_TREES, "L": L_TREES, "S": S_TREES}
    receive = {"R": r_recv, "L": l_recv, "S": s_recv}
    number = {"R": 0, "L": 1, "S": 2}

    def start_one(name, message, piece, link, child, index):
        device = place.col_neighbour(link) if name == "L" else place.row_neighbour(link)
        sem = cols_send.at[number[name]] if piece is COLS else send.at[number[name]]
        to = ref_of(name, child, piece) if name == "S" else None
        remote(ref_of(name, message, piece), sem, receive[name].at[index, slot(child)], device, to).start()

    def send_on(name, message, piece):
        for link, child in trees[name][piece][message]:
            start_one(name, message, piece, link, child, piece)

    def arrive(name, message, piece):
        remote(
            ref_of(name, message, piece), send.at[number[name]], receive[name].at[piece, slot(message)], sibling
        ).wait_recv()
        send_on(name, message, piece)

    sib_sems = {"R": (r_sib, 3), "S": (s_sib, 4)}

    def chunk(name, message, core):
        if name == "S":
            return sp[slot(message)].at[core]
        return rp.at[place.row_source(message) // 2 * 2 + core]

    def to_sibling(name, message):
        sem, n = sib_sems[name]
        remote(chunk(name, message, place.core), send.at[n], sem.at[slot(message)], sibling).start()

    def from_sibling(name, message):
        sem, n = sib_sems[name]
        remote(chunk(name, message, 1 - place.core), send.at[n], sem.at[slot(message)], sibling).wait_recv()

    mine = pc.at[q, place.core]
    other = pc.at[q, 1 - place.core]
    remote(mine, cols_send.at[3], pair_sem.at[0], sibling).start()
    for k in range(PIECES):
        send_on("R", OWN, k)
        send_on("L", OWN, k)
    send_on("L", OWN, COLS)
    to_sibling("R", OWN)
    remote(other, cols_send.at[3], pair_sem.at[0], sibling).wait_recv()
    send_on("R", OWN, COLS)

    left = {m: PIECES for m in MESSAGES}
    for _, name, message, piece in plan([("R", R_TREES, R_LINKS), ("L", L_TREES, L_LINKS)]):
        arrive(name, message, piece)
        if name == "R" and piece != COLS:
            left[message] -= 1
            if left[message] == 0:
                to_sibling("R", message)

    copies = [
        pltpu.make_async_copy(pc, pc_s, local_sem.at[0]),
        pltpu.make_async_copy(lc, lc_s, local_sem.at[1]),
    ]
    for copy in copies:
        copy.start()
    for copy in copies:
        copy.wait()
    for message in MESSAGES:
        from_sibling("R", message)

    def wanted(i):
        js = [cs_ref[i * KC + s] for s in range(KC)]
        return [jnp.where(j >= 0, j, -2) for j in js]

    def split(v):
        hi = v.astype(jnp.bfloat16)
        return hi, (v - hi.astype(jnp.float32)).astype(jnp.bfloat16)

    def group_product(i, g, block, js):
        high, low = [], []
        for t in range(KC):
            m = jnp.maximum(lc_s[g, 0, i * KC + t], 0)
            core, row = m // ROWS % 2, m % ROWS
            held = [pc_s[g, core, 0, row * KC + u] for u in range(KC)]
            tiles = []
            for h in range(2):
                moved, found = [], []
                for s in (2 * h, 2 * h + 1):
                    j = js[s]
                    hit = [v == j for v in held]
                    half = jnp.where(hit[2] | hit[3], 1, 0)
                    odd = jnp.where(hit[1] | hit[3], 1, 0)
                    found.append(hit[0] | hit[1] | hit[2] | hit[3])
                    v = block(g, core, row, half)
                    shift = odd * 64 if s % 2 == 0 else 64 - odd * 64
                    moved.append(pltpu.roll(v, shift, 1))
                below = jnp.where(found[0], 64, 0)
                above = jnp.where(found[1], 64, 128)
                tiles.append(jnp.where(lane < below, moved[0], jnp.where(lane >= above, moved[1], 0.0)))
            hi, lo = split(jnp.concatenate(tiles, axis=1))
            high.append(hi)
            low.append(lo)
        w_hi = jnp.concatenate(high, axis=0)
        w_lo = jnp.concatenate(low, axis=0)
        a_hi, a_lo = split(jnp.concatenate([lp[g, i, 0], lp[g, i, 1]], axis=1))
        first = jnp.dot(jnp.concatenate([a_hi, a_lo], axis=0), w_hi, preferred_element_type=jnp.float32)
        second = jnp.dot(a_hi, w_lo, preferred_element_type=jnp.float32)
        return first[:64] + first[64:] + second

    def store_slots(out_ref, panel, i):
        for h in range(2):
            even = panel[h, pl.ds(0, 32, stride=2), :]
            odd = panel[h, pl.ds(1, 32, stride=2), :]
            out_ref[i, pl.ds(2 * h, 32, stride=4), :] = jnp.where(lane_half, even, pltpu.roll(odd, 64, 1))
            out_ref[i, pl.ds(2 * h + 1, 32, stride=4), :] = jnp.where(lane_half, pltpu.roll(even, 64, 1), odd)

    def square_piece(k, carry):
        def square_row(n, inner):
            i = k * STEP + n
            js = wanted(i)

            def add(g, total):
                return total + group_product(i, g, lambda g, core, row, half: rp[g * 2 + core, row, half], js)

            total = lax.fori_loop(0, N_C, add, jnp.zeros((64, 256), jnp.float32), unroll=8)
            sp[0][place.core, i, 0] = total[:, :128]
            sp[0][place.core, i, 1] = total[:, 128:]
            store_slots(sq_ref, sp[0].at[place.core, i], i)
            return inner

        lax.fori_loop(0, STEP, square_row, 0)
        for link, child in (("+", (1, 0)), ("-", (3, 0)), ("pair", (0, 1))):
            start_one("S", OWN, k, link, child, k)
        return carry

    lax.fori_loop(0, PIECES, square_piece, 0)
    to_sibling("S", OWN)

    def update_source(message, first):
        g = place.row_source(message) // 2
        panel = sp[slot(message)]

        def update_row(i, carry):
            total = group_product(i, g, lambda g, core, row, half: panel[core, row, half], wanted(i))
            if not first:
                total = total + jnp.concatenate([acc[i, 0], acc[i, 1]], axis=1)
            acc[i, 0] = total[:, :128]
            acc[i, 1] = total[:, 128:]
            return carry

        lax.fori_loop(0, ROWS, update_row, 0, unroll=2)

    events = [(t, "arrive", m, k) for t, _, m, k in plan([("S", S_TREES, R_LINKS)]) if k != COLS]
    done = {m: max(t for t, _, n, _ in events if n == m) for m in MESSAGES if m != OWN}
    done[OWN] = 0.0
    events += [(t, "share", m, 0) for m, t in done.items() if m != OWN]
    events += [(t + 4.0, "use", m, 0) for m, t in done.items()]
    used = 0
    for _, kind, message, piece in sorted(events, key=lambda e: e[0]):
        if kind == "arrive":
            arrive("S", message, piece)
        elif kind == "share":
            to_sibling("S", message)
        else:
            from_sibling("S", message)
            update_source(message, used == 0)
            used += 1

    def finish(i, carry):
        for h in range(2):
            acc[i, h] = 1.5 * rp[r, i, h] - 0.5 * acc[i, h]
        store_slots(up_ref, acc.at[i], i)
        return carry

    lax.fori_loop(0, ROWS, finish, 0)

    for name in ("R", "L", "S"):
        remote(rp.at[pl.ds(0, 7)], send.at[number[name]], receive[name].at[0, 0], sibling).wait_send()
    for name in ("R", "S"):
        sem, n = sib_sems[name]
        remote(rp.at[pl.ds(0, 8)], send.at[n], sem.at[0], sibling).wait_send()
    remote(pc.at[pl.ds(0, 7)], cols_send.at[0], r_recv.at[0, 0], sibling).wait_send()
    remote(lc.at[pl.ds(0, 7)], cols_send.at[1], l_recv.at[0, 0], sibling).wait_send()
    remote(mine, cols_send.at[3], pair_sem.at[0], sibling).wait_send()


def local(x_blocks, block_cols):
    x = x_blocks.reshape(ROWS, KC, 32, 128).transpose(0, 2, 1, 3).reshape(ROWS, 128, 128)
    flat = block_cols.reshape(ROWS * KC)
    tile = jnp.zeros((8, 128), jnp.int32).at[0, : ROWS * KC].set(flat)
    out = jax.ShapeDtypeStruct((ROWS, 128, 128), jnp.float32)
    vmem = pl.BlockSpec(memory_space=pltpu.VMEM)
    dma = pltpu.SemaphoreType.DMA
    square, updated = pl.pallas_call(
        kernel,
        out_shape=(out, out),
        in_specs=[vmem, vmem, pl.BlockSpec(memory_space=pltpu.SMEM)],
        out_specs=(vmem, vmem),
        scratch_shapes=[
            pltpu.VMEM((N_R, ROWS, 2, 64, 128), jnp.float32),
            pltpu.VMEM((N_C, ROWS, 2, 64, 128), jnp.float32),
            pltpu.VMEM((ROWS, 2, 64, 128), jnp.float32),
            pltpu.VMEM((N_R // 2, 2, 8, 128), jnp.int32),
            pltpu.VMEM((N_C, 8, 128), jnp.int32),
            pltpu.SMEM((N_R // 2, 2, 8, 128), jnp.int32),
            pltpu.SMEM((N_C, 8, 128), jnp.int32),
            dma((5,)),
            dma((4,)),
            dma((PIECES + 1, 8)),
            dma((PIECES + 1, 8)),
            dma((PIECES + 1, 8)),
            dma((8,)),
            dma((8,)),
            dma((1,)),
            dma((2,)),
        ]
        + [pltpu.VMEM((2, ROWS, 2, 64, 128), jnp.float32)] * 8,
        compiler_params=pltpu.CompilerParams(
            collective_id=0, has_side_effects=True, vmem_limit_bytes=56 << 20
        ),
        cost_estimate=pl.CostEstimate(flops=1 << 30, bytes_accessed=4 << 20, transcendentals=0),
    )(x, tile, flat)

    def back(y):
        return y.reshape(ROWS, 32, KC, 128).transpose(0, 2, 1, 3).reshape(ROWS, KC, 4096)

    return back(square), back(updated)


def solution(mesh):
    return jax.shard_map(
        local,
        mesh=mesh,
        in_specs=(P("row", "col", None), P("row", "col")),
        out_specs=(P("row", "col", None), P("row", "col", None)),
        check_vma=False,
    )
```

```python
import heapq

import jax
import jax.numpy as jnp
from jax import lax
from jax.experimental import pallas as pl
from jax.experimental.pallas import tpu as pltpu
from jax.sharding import PartitionSpec as P

MESH = pl.DeviceIdType.MESH

ROWS = 16
KC = 4
N_R = 16
N_C = 8
PIECES = 8
STEP = ROWS // PIECES
PIECE_US = 23.0 / PIECES
HOP_US = 1.5
R_GAP, L_GAP, S_GAP = 3.0, 8.0, 2.0
CHUNK = 2 * ROWS
SPAN = 2 * CHUNK + 1
ZERO = 2 * CHUNK
COLS = PIECES

OWN = (0, 0)
MESSAGES = [(d, p) for d in range(4) for p in range(2)]


def slot(message):
    return message[0] * 2 + message[1]


def tree(piece, pair_first):
    def route(message):
        d, p = message
        if d == 2:
            forward = (piece + (p if pair_first else 0)) % 2 == 0
            ring = ["+", "+"] if forward else ["-", "-"]
        else:
            ring = [[], ["+"], None, ["-"]][d]
        pair = ["pair"] * p
        return tuple(pair + ring if pair_first else ring + pair)

    by_route = {route(m): m for m in MESSAGES}
    children = {m: [] for m in MESSAGES}
    for m in MESSAGES:
        if m != OWN:
            r = route(m)
            children[by_route[r[:-1]]].append((r[-1], m))
    return children


def plan(gathers):
    free = {}
    order = []
    queue = []
    count = 0
    for name, trees, links, gap in gathers:
        for piece in [COLS] + list(range(PIECES)):
            count += 1
            heapq.heappush(queue, (gap * piece if piece != COLS else 0.0, count, name, OWN, piece))
    table = {name: (trees, links) for name, trees, links, _ in gathers}
    while queue:
        now, _, name, message, piece = heapq.heappop(queue)
        order.append((now, name, message, piece))
        trees, links = table[name]
        for link, child in trees[piece][message]:
            wire = links[link]
            start = max(now, free.get(wire, 0.0))
            free[wire] = start + (0.05 if piece == COLS else PIECE_US)
            count += 1
            heapq.heappush(queue, (free[wire] + HOP_US, count, name, child, piece))
    return sorted(order, key=lambda e: e[0])


def trees_of(pair_first):
    return [tree(k, pair_first[k]) for k in range(PIECES)] + [tree(0, True)]


R_TREES = trees_of([k % 4 != 3 for k in range(PIECES)])
L_TREES = trees_of([True] * PIECES)
S_TREES = trees_of([k % 8 not in (2, 5, 7) for k in range(PIECES)])
R_LINKS = {"+": "x+", "-": "x-", "pair": "y"}
L_LINKS = {"+": "z+", "-": "z-", "pair": "y"}


class Place:
    def __init__(self):
        self.r = lax.axis_index("row")
        self.c = lax.axis_index("col")
        self.core = self.r % 2
        self.x = (self.r // 2) % 4
        self.yl = self.r // 8
        self.z = self.c // 2
        self.yh = self.c % 2
        self.q = self.r // 2

    def row_of(self, x, yl, core):
        return (yl * 4 + x) * 2 + core

    def row_source(self, message):
        d, p = message
        yl = 1 - self.yl if p else self.yl
        return self.row_of((self.x + 4 - d) % 4, yl, self.core)

    def col_source(self, message):
        d, p = message
        yh = 1 - self.yh if p else self.yh
        return ((self.z + 4 - d) % 4) * 2 + yh

    def row_neighbour(self, link):
        if link == "pair":
            return (self.row_of(self.x, 1 - self.yl, self.core), self.c)
        return (self.row_of((self.x + (1 if link == "+" else 3)) % 4, self.yl, self.core), self.c)

    def col_neighbour(self, link):
        if link == "pair":
            return (self.r, self.z * 2 + 1 - self.yh)
        return (self.r, ((self.z + (1 if link == "+" else 3)) % 4) * 2 + self.yh)

    def sibling(self):
        return (self.row_of(self.x, self.yl, 1 - self.core), self.c)


def remote(ref, send, recv, device, to=None):
    return pltpu.make_async_remote_copy(
        src_ref=ref,
        dst_ref=ref if to is None else to,
        send_sem=send,
        recv_sem=recv,
        device_id=device,
        device_id_type=MESH,
    )


def kernel(
    x_ref, tile_ref, cs_ref, sq_ref, up_ref,
    rp, lp, acc, pc, lc, pc_s, lc_s, at_s, low_s, high_s,
    send, cols_send, r_recv, l_recv, s_recv, r_sib, s_sib, pair_sem, local_sem,
    *sp,
):
    place = Place()
    r, c, q = place.r, place.c, place.q
    sibling = place.sibling()
    lane = lax.broadcasted_iota(jnp.int32, (64, 128), 1)
    lane_half = lax.broadcasted_iota(jnp.int32, (32, 128), 1) < 64
    home = q * SPAN + place.core * CHUNK

    barrier = pltpu.get_barrier_semaphore()
    neighbours = [place.row_neighbour(k) for k in ("+", "-", "pair")]
    neighbours += [place.col_neighbour(k) for k in ("+", "-", "pair")] + [sibling]
    for device in neighbours:
        pl.semaphore_signal(barrier, inc=1, device_id=device, device_id_type=MESH)

    def convert(i, carry):
        for h in range(2):
            pair = []
            for u in (2 * h, 2 * h + 1):
                v = x_ref[i, pl.ds(u, 32, stride=4), :]
                pair.append(jnp.where(cs_ref[i * KC + u] >= 0, v, 0.0))
            even = jnp.where(lane_half, pair[0], pltpu.roll(pair[1], 64, 1))
            odd = jnp.where(lane_half, pltpu.roll(pair[0], 64, 1), pair[1])
            for n, part in enumerate((even, odd)):
                rp[home + 2 * i + h, pl.ds(n, 32, stride=2), :] = part
                lp[c, i, h, pl.ds(n, 32, stride=2), :] = part
        return carry

    lax.fori_loop(0, ROWS, convert, 0)
    for n in range(8):
        rp[n * SPAN + ZERO] = jnp.zeros((64, 128), jnp.float32)
        sp[n][ZERO] = jnp.zeros((64, 128), jnp.float32)
    pc[q, place.core] = tile_ref[...]
    lc[c] = tile_ref[...]
    pl.semaphore_wait(barrier, len(neighbours))

    def ref_of(name, message, piece, core=None):
        if name == "L":
            n = place.col_source(message)
            return lc.at[n] if piece == COLS else lp.at[n, pl.ds(piece * STEP, STEP)]
        first = (place.core if core is None else core) * CHUNK
        chip = place.row_source(message) // 2
        if name == "R" and piece == COLS:
            return pc.at[chip]
        n = CHUNK
        if piece is not None:
            first, n = first + piece * 2 * STEP, 2 * STEP
        if name == "S":
            return sp[slot(message)].at[pl.ds(first, n)]
        return rp.at[pl.ds(chip * SPAN + first, n)]

    trees = {"R": R_TREES, "L": L_TREES, "S": S_TREES}
    receive = {"R": r_recv, "L": l_recv, "S": s_recv}
    number = {"R": 0, "L": 1, "S": 2}

    def start_one(name, message, piece, link, child, index):
        device = place.col_neighbour(link) if name == "L" else place.row_neighbour(link)
        sem = cols_send.at[number[name]] if piece is COLS else send.at[number[name]]
        to = ref_of(name, child, piece) if name == "S" else None
        remote(ref_of(name, message, piece), sem, receive[name].at[index, slot(child)], device, to).start()

    def send_on(name, message, piece):
        for link, child in trees[name][piece][message]:
            start_one(name, message, piece, link, child, piece)

    def arrive(name, message, piece):
        remote(
            ref_of(name, message, piece), send.at[number[name]], receive[name].at[piece, slot(message)], sibling
        ).wait_recv()
        send_on(name, message, piece)
        if name != "L" and piece != COLS:
            to_sibling(name, message, piece)

    sib_sems = {"R": (r_sib, 3), "S": (s_sib, 4)}

    def to_sibling(name, message, piece):
        sem, n = sib_sems[name]
        remote(ref_of(name, message, piece), send.at[n], sem.at[slot(message)], sibling).start()

    def from_sibling(name, message):
        sem, n = sib_sems[name]
        whole = ref_of(name, message, None, 1 - place.core)
        remote(whole, send.at[n], sem.at[slot(message)], sibling).wait_recv()

    mine = pc.at[q, place.core]
    other = pc.at[q, 1 - place.core]
    remote(mine, cols_send.at[3], pair_sem.at[0], sibling).start()
    send_on("L", OWN, COLS)
    remote(other, cols_send.at[3], pair_sem.at[0], sibling).wait_recv()
    send_on("R", OWN, COLS)

    def load_columns():
        copies = [
            pltpu.make_async_copy(pc, pc_s, local_sem.at[0]),
            pltpu.make_async_copy(lc, lc_s, local_sem.at[1]),
        ]
        for copy in copies:
            copy.start()
        for copy in copies:
            copy.wait()

    def find_row(i, carry):
        js = [cs_ref[i * KC + s] for s in range(KC)]
        js = [jnp.where(j >= 0, j, -2) for j in js]

        def find(n, inner):
            m = lc_s[n // KC, 0, i * KC + n % KC]
            there = jnp.maximum(m, 0)
            core, row = there // ROWS % 2, there % ROWS
            held = [pc_s[n // KC, core, 0, row * KC + u] for u in range(KC)]
            start = (core * ROWS + row) * 2
            spot = i * 32 + n
            for s in range(KC):
                hit = [v == js[s] for v in held]
                at = jnp.where(hit[0] | hit[1], start, jnp.where(hit[2] | hit[3], start + 1, ZERO))
                at_s[spot * KC + s] = jnp.where(m >= 0, at, ZERO)
                odd = hit[1] | hit[3]
                if s % 2 == 0:
                    low_s[spot * 2 + s // 2] = jnp.where(odd, 64, 0)
                else:
                    high_s[spot * 2 + s // 2] = jnp.where(odd, 128, 64)
            return inner

        return lax.fori_loop(0, 32, find, carry, unroll=4)

    def find_rows(n):
        lax.fori_loop(n * 4, n * 4 + 4, find_row, 0)

    events = [
        (t, name, m, k)
        for t, name, m, k in plan([("R", R_TREES, R_LINKS, R_GAP), ("L", L_TREES, L_LINKS, L_GAP)])
        if not (m == OWN and k == COLS)
    ]
    known = max(t for t, _, _, k in events if k == COLS)
    events += [(known + 0.1 + 4.0 * n, "find", None, n) for n in range(4)]
    events.sort(key=lambda e: e[0])
    ready = max(t for t, name, _, _ in events if name != "L")

    def follow(some):
        for _, name, message, piece in some:
            if name == "find":
                if piece == 0:
                    load_columns()
                find_rows(piece)
            elif message == OWN:
                send_on(name, message, piece)
                if name == "R":
                    to_sibling(name, message, piece)
            else:
                arrive(name, message, piece)

    follow([e for e in events if e[0] <= ready])
    late = [e for e in events if e[0] > ready]
    for message in MESSAGES:
        from_sibling("R", message)

    def split(v):
        hi = v.astype(jnp.bfloat16)
        return hi, (v - hi.astype(jnp.float32)).astype(jnp.bfloat16)

    left_half = lane < 64

    def group_product(i, g, block):
        high, low = [], []
        for t in range(KC):
            spot = i * 32 + g * KC + t
            tiles = []
            for h in range(2):
                one = block(at_s[spot * KC + 2 * h])
                two = block(at_s[spot * KC + 2 * h + 1])
                kept = (lane >= low_s[spot * 2 + h]) & (lane < high_s[spot * 2 + h])
                straight = jnp.where(left_half, one, two)
                swapped = pltpu.roll(jnp.where(left_half, two, one), 64, 1)
                tiles.append(jnp.where(kept, straight, swapped))
            hi, lo = split(jnp.concatenate(tiles, axis=1))
            high.append(hi)
            low.append(lo)
        w_hi = jnp.concatenate(high, axis=0)
        w_lo = jnp.concatenate(low, axis=0)
        a_hi, a_lo = split(jnp.concatenate([lp[g, i, 0], lp[g, i, 1]], axis=1))
        first = jnp.dot(jnp.concatenate([a_hi, a_lo], axis=0), w_hi, preferred_element_type=jnp.float32)
        second = jnp.dot(a_hi, w_lo, preferred_element_type=jnp.float32)
        return first[:64] + first[64:] + second

    def store_slots(out_ref, i, read):
        for h in range(2):
            even = read(h, pl.ds(0, 32, stride=2))
            odd = read(h, pl.ds(1, 32, stride=2))
            out_ref[i, pl.ds(2 * h, 32, stride=4), :] = jnp.where(lane_half, even, pltpu.roll(odd, 64, 1))
            out_ref[i, pl.ds(2 * h + 1, 32, stride=4), :] = jnp.where(lane_half, pltpu.roll(even, 64, 1), odd)

    def square_piece(k, carry):
        def square_row(n, inner):
            i = k * STEP + n

            def add(g, total):
                return total + group_product(i, g, lambda at: rp[g * SPAN + at])

            total = lax.fori_loop(0, N_C, add, jnp.zeros((64, 256), jnp.float32), unroll=8)
            spot = place.core * CHUNK + 2 * i
            sp[0][spot] = total[:, :128]
            sp[0][spot + 1] = total[:, 128:]
            store_slots(sq_ref, i, lambda h, rows: sp[0][spot + h, rows, :])
            return inner

        lax.fori_loop(0, STEP, square_row, 0)
        for link, child in (("+", (1, 0)), ("-", (3, 0)), ("pair", (0, 1))):
            start_one("S", OWN, k, link, child, k)
        to_sibling("S", OWN, k)
        return carry

    full = min([PIECES] + [k for _, _, _, k in late])
    lax.fori_loop(0, full, square_piece, 0)
    for k in range(full, PIECES):
        needed = [n for n, e in enumerate(late) if e[3] <= k]
        if needed:
            follow(late[: needed[-1] + 1])
            late = late[needed[-1] + 1 :]
        square_piece(k, 0)

    def update_source(message, first):
        g = place.row_source(message) // 2
        panel = sp[slot(message)]

        def update_row(i, carry):
            total = group_product(i, g, lambda at: panel[at])
            if not first:
                total = total + jnp.concatenate([acc[i, 0], acc[i, 1]], axis=1)
            acc[i, 0] = total[:, :128]
            acc[i, 1] = total[:, 128:]
            return carry

        lax.fori_loop(0, ROWS, update_row, 0, unroll=4)

    events = [(t, "arrive", m, k) for t, _, m, k in plan([("S", S_TREES, R_LINKS, S_GAP)]) if k != COLS and m != OWN]
    done = {m: max(t for t, _, n, _ in events if n == m) for m in MESSAGES if m != OWN}
    events += [(t + 1.5, "use", m, 0) for m, t in done.items()] + [(2.0, "use", OWN, 0)]
    used = 0
    for _, kind, message, piece in sorted(events, key=lambda e: e[0]):
        if kind == "arrive":
            arrive("S", message, piece)
        else:
            from_sibling("S", message)
            update_source(message, used == 0)
            used += 1

    def finish(i, carry):
        for h in range(2):
            acc[i, h] = 1.5 * rp[home + 2 * i + h] - 0.5 * acc[i, h]
        store_slots(up_ref, i, lambda h, rows: acc[i, h, rows, :])
        return carry

    lax.fori_loop(0, ROWS, finish, 0)

    for name in ("R", "L", "S"):
        remote(rp.at[pl.ds(0, 7 * CHUNK)], send.at[number[name]], receive[name].at[0, 0], sibling).wait_send()
    for name in ("R", "S"):
        sem, n = sib_sems[name]
        remote(rp.at[pl.ds(0, 8 * CHUNK)], send.at[n], sem.at[0], sibling).wait_send()
    remote(pc.at[pl.ds(0, 7)], cols_send.at[0], r_recv.at[0, 0], sibling).wait_send()
    remote(lc.at[pl.ds(0, 7)], cols_send.at[1], l_recv.at[0, 0], sibling).wait_send()
    remote(mine, cols_send.at[3], pair_sem.at[0], sibling).wait_send()


def local(x_blocks, block_cols):
    x = x_blocks.reshape(ROWS, KC, 32, 128).transpose(0, 2, 1, 3).reshape(ROWS, 128, 128)
    flat = block_cols.reshape(ROWS * KC)
    tile = jnp.zeros((8, 128), jnp.int32).at[0, : ROWS * KC].set(flat)
    out = jax.ShapeDtypeStruct((ROWS, 128, 128), jnp.float32)
    vmem = pl.BlockSpec(memory_space=pltpu.VMEM)
    dma = pltpu.SemaphoreType.DMA
    square, updated = pl.pallas_call(
        kernel,
        out_shape=(out, out),
        in_specs=[vmem, vmem, pl.BlockSpec(memory_space=pltpu.SMEM)],
        out_specs=(vmem, vmem),
        scratch_shapes=[
            pltpu.VMEM((N_R // 2 * SPAN, 64, 128), jnp.float32),
            pltpu.VMEM((N_C, ROWS, 2, 64, 128), jnp.float32),
            pltpu.VMEM((ROWS, 2, 64, 128), jnp.float32),
            pltpu.VMEM((N_R // 2, 2, 8, 128), jnp.int32),
            pltpu.VMEM((N_C, 8, 128), jnp.int32),
            pltpu.SMEM((N_R // 2, 2, 8, 128), jnp.int32),
            pltpu.SMEM((N_C, 8, 128), jnp.int32),
            pltpu.SMEM((ROWS * 32 * KC,), jnp.int32),
            pltpu.SMEM((ROWS * 32 * 2,), jnp.int32),
            pltpu.SMEM((ROWS * 32 * 2,), jnp.int32),
            dma((5,)),
            dma((4,)),
            dma((PIECES + 1, 8)),
            dma((PIECES + 1, 8)),
            dma((PIECES + 1, 8)),
            dma((8,)),
            dma((8,)),
            dma((1,)),
            dma((2,)),
        ]
        + [pltpu.VMEM((SPAN, 64, 128), jnp.float32)] * 8,
        compiler_params=pltpu.CompilerParams(
            collective_id=0, has_side_effects=True, vmem_limit_bytes=56 << 20
        ),
        cost_estimate=pl.CostEstimate(flops=1 << 30, bytes_accessed=4 << 20, transcendentals=0),
    )(x, tile, flat)

    def back(y):
        return y.reshape(ROWS, 32, KC, 128).transpose(0, 2, 1, 3).reshape(ROWS, KC, 4096)

    return back(square), back(updated)


def solution(mesh):
    return jax.shard_map(
        local,
        mesh=mesh,
        in_specs=(P("row", "col", None), P("row", "col")),
        out_specs=(P("row", "col", None), P("row", "col", None)),
        check_vma=False,
    )
```

```python
import heapq

import jax
import jax.numpy as jnp
from jax import lax
from jax.experimental import pallas as pl
from jax.experimental.pallas import tpu as pltpu
from jax.sharding import PartitionSpec as P

MESH = pl.DeviceIdType.MESH

ROWS = 16
KC = 4
N_R = 16
N_C = 8
PIECES = 8
STEP = ROWS // PIECES
PIECE_US = 23.0 / PIECES
HOP_US = 1.5
FIND_GAP = 2.5
SQUARE_US = 1.1
R_GAP, L_GAP = 3.0, 6.0
CHUNK = 2 * ROWS
SPAN = 2 * CHUNK + 1
ZERO = 2 * CHUNK
TOGETHER = 4
GROUP = 4
COLS = PIECES

OWN = (0, 0)
MESSAGES = [(d, p) for d in range(4) for p in range(2)]


def slot(message):
    return message[0] * 2 + message[1]


def tree(piece, pair_first):
    def route(message):
        d, p = message
        if d == 2:
            forward = (piece + (p if pair_first else 0)) % 2 == 0
            ring = ["+", "+"] if forward else ["-", "-"]
        else:
            ring = [[], ["+"], None, ["-"]][d]
        pair = ["pair"] * p
        return tuple(pair + ring if pair_first else ring + pair)

    by_route = {route(m): m for m in MESSAGES}
    children = {m: [] for m in MESSAGES}
    for m in MESSAGES:
        if m != OWN:
            r = route(m)
            children[by_route[r[:-1]]].append((r[-1], m))
    return children


def plan(gathers):
    free = {}
    order = []
    queue = []
    count = 0
    for name, trees, links, starts in gathers:
        for piece in [COLS] + list(range(PIECES)):
            count += 1
            heapq.heappush(queue, (starts[piece] if piece != COLS else 0.0, count, name, OWN, piece))
    table = {name: (trees, links) for name, trees, links, _ in gathers}
    while queue:
        now, _, name, message, piece = heapq.heappop(queue)
        order.append((now, name, message, piece))
        trees, links = table[name]
        for link, child in trees[piece][message]:
            wire = links[link]
            start = max(now, free.get(wire, 0.0))
            free[wire] = start + (0.05 if piece == COLS else PIECE_US)
            count += 1
            heapq.heappush(queue, (free[wire] + HOP_US, count, name, child, piece))
    return sorted(order, key=lambda e: e[0])


def trees_of(pair_first):
    return [tree(k, pair_first[k]) for k in range(PIECES)] + [tree(0, True)]


R_TREES = trees_of([k not in (2, 3) for k in range(PIECES)])
L_TREES = trees_of([True] * PIECES)
S_TREES = trees_of([k % 8 not in (2, 5, 7) for k in range(PIECES)])
R_LINKS = {"+": "x+", "-": "x-", "pair": "y"}
L_LINKS = {"+": "z+", "-": "z-", "pair": "y"}


def whole_plan():
    first = [
        ("R", R_TREES, R_LINKS, [R_GAP * k for k in range(PIECES)]),
        ("L", L_TREES, L_LINKS, [L_GAP * k for k in range(PIECES)]),
    ]
    steps = plan(first)
    ready = max(t for t, name, _, _ in steps if name == "R")
    starts, now = [], ready + 2.0
    for k in range(PIECES):
        now = max(now, max(t for t, name, _, n in steps if name == "L" and n <= k) + 0.5) + SQUARE_US
        starts.append(now)
    steps = plan(first + [("S", S_TREES, R_LINKS, starts)])
    known = max(t for t, name, _, n in steps if name != "S" and n == COLS)
    events = [(known + 0.1 + FIND_GAP * n, "find", "", None, n) for n in range(ROWS)]
    done = {}
    for t, name, message, piece in steps:
        if name == "S" and piece == COLS or message == OWN and name != "S" and piece in (COLS, 0):
            continue
        if message != OWN:
            events.append((t, "arrive", name, message, piece))
            if name == "S":
                done[message] = max(t, done.get(message, 0.0))
        elif name == "S":
            events.append((t - SQUARE_US, "square", name, message, piece))
        else:
            events.append((t, "send", name, message, piece))
    events += [(t + 1.5, "use", "S", message, 0) for message, t in done.items()]
    events.append((starts[-1] + 0.1, "use", "S", OWN, 0))
    events.sort(key=lambda e: e[0])
    return [e[1:] for e in events]


class Place:
    def __init__(self):
        self.r = lax.axis_index("row")
        self.c = lax.axis_index("col")
        self.core = self.r % 2
        self.x = (self.r // 2) % 4
        self.yl = self.r // 8
        self.z = self.c // 2
        self.yh = self.c % 2
        self.q = self.r // 2

    def row_of(self, x, yl, core):
        return (yl * 4 + x) * 2 + core

    def row_source(self, message):
        d, p = message
        yl = 1 - self.yl if p else self.yl
        return self.row_of((self.x + 4 - d) % 4, yl, self.core)

    def col_source(self, message):
        d, p = message
        yh = 1 - self.yh if p else self.yh
        return ((self.z + 4 - d) % 4) * 2 + yh

    def row_neighbour(self, link):
        if link == "pair":
            return (self.row_of(self.x, 1 - self.yl, self.core), self.c)
        return (self.row_of((self.x + (1 if link == "+" else 3)) % 4, self.yl, self.core), self.c)

    def col_neighbour(self, link):
        if link == "pair":
            return (self.r, self.z * 2 + 1 - self.yh)
        return (self.r, ((self.z + (1 if link == "+" else 3)) % 4) * 2 + self.yh)

    def sibling(self):
        return (self.row_of(self.x, self.yl, 1 - self.core), self.c)


def remote(ref, send, recv, device, to=None):
    return pltpu.make_async_remote_copy(
        src_ref=ref,
        dst_ref=ref if to is None else to,
        send_sem=send,
        recv_sem=recv,
        device_id=device,
        device_id_type=MESH,
    )


def kernel(
    x_ref, cols_ref, cs_ref, sq_ref, up_ref,
    rp, lp, acc, pc, lc, pc_s, lc_s, at_s, low_s, high_s,
    send, cols_send, r_recv, l_recv, s_recv, r_sib, s_sib, pair_sem, local_sem,
    *sp,
):
    place = Place()
    r, c, q = place.r, place.c, place.q
    sibling = place.sibling()
    lane = lax.broadcasted_iota(jnp.int32, (64, 128), 1)
    lane_half = lax.broadcasted_iota(jnp.int32, (32, 128), 1) < 64
    home = q * SPAN + place.core * CHUNK

    barrier = pltpu.get_barrier_semaphore()
    neighbours = [place.row_neighbour(k) for k in ("+", "-", "pair")]
    neighbours += [place.col_neighbour(k) for k in ("+", "-", "pair")] + [sibling]
    for device in neighbours:
        pl.semaphore_signal(barrier, inc=1, device_id=device, device_id_type=MESH)

    def convert(i, carry):
        for h in range(2):
            pair = []
            for u in (2 * h, 2 * h + 1):
                v = x_ref[i, pl.ds(u, 32, stride=4), :]
                pair.append(jnp.where(cs_ref[u, i] >= 0, v, 0.0))
            even = jnp.where(lane_half, pair[0], pltpu.roll(pair[1], 64, 1))
            odd = jnp.where(lane_half, pltpu.roll(pair[0], 64, 1), pair[1])
            for n, part in enumerate((even, odd)):
                rp[home + 2 * i + h, pl.ds(n, 32, stride=2), :] = part
                lp[c, i, h, pl.ds(n, 32, stride=2), :] = part
        return carry

    lax.fori_loop(0, ROWS, convert, 0)
    for n in range(8):
        rp[n * SPAN + ZERO] = jnp.zeros((64, 128), jnp.float32)
        sp[n][ZERO] = jnp.zeros((64, 128), jnp.float32)
    for tile in (pc.at[q, place.core], lc.at[c]):
        tile[...] = jnp.zeros((8, 128), jnp.int32)
        tile[:KC, :ROWS] = cols_ref[...]
    pl.semaphore_wait(barrier, len(neighbours))

    def ref_of(name, message, piece, core=None):
        if name == "L":
            n = place.col_source(message)
            return lc.at[n] if piece == COLS else lp.at[n, pl.ds(piece * STEP, STEP)]
        first = (place.core if core is None else core) * CHUNK
        chip = place.row_source(message) // 2
        if name == "R" and piece == COLS:
            return pc.at[chip]
        n = CHUNK
        if piece is not None:
            first, n = first + piece * 2 * STEP, 2 * STEP
        if name == "S":
            return sp[slot(message)].at[pl.ds(first, n)]
        return rp.at[pl.ds(chip * SPAN + first, n)]

    trees = {"R": R_TREES, "L": L_TREES, "S": S_TREES}
    receive = {"R": r_recv, "L": l_recv, "S": s_recv}
    number = {"R": 0, "L": 1, "S": 2}

    def start_one(name, message, piece, link, child, index):
        device = place.col_neighbour(link) if name == "L" else place.row_neighbour(link)
        sem = cols_send.at[number[name]] if piece is COLS else send.at[number[name]]
        to = ref_of(name, child, piece) if name == "S" else None
        remote(ref_of(name, message, piece), sem, receive[name].at[index, slot(child)], device, to).start()

    def send_on(name, message, piece):
        for link, child in trees[name][piece][message]:
            start_one(name, message, piece, link, child, piece)

    def arrive(name, message, piece):
        remote(
            ref_of(name, message, piece), send.at[number[name]], receive[name].at[piece, slot(message)], sibling
        ).wait_recv()
        send_on(name, message, piece)
        if name != "L" and piece != COLS:
            to_sibling(name, message, piece)

    sib_sems = {"R": (r_sib, 3), "S": (s_sib, 4)}

    def to_sibling(name, message, piece):
        sem, n = sib_sems[name]
        remote(ref_of(name, message, piece), send.at[n], sem.at[slot(message)], sibling).start()

    def from_sibling(name, message):
        sem, n = sib_sems[name]
        whole = ref_of(name, message, None, 1 - place.core)
        remote(whole, send.at[n], sem.at[slot(message)], sibling).wait_recv()

    mine = pc.at[q, place.core]
    other = pc.at[q, 1 - place.core]
    remote(mine, cols_send.at[3], pair_sem.at[0], sibling).start()
    send_on("L", OWN, COLS)
    send_on("R", OWN, 0)
    send_on("L", OWN, 0)
    to_sibling("R", OWN, 0)
    remote(other, cols_send.at[3], pair_sem.at[0], sibling).wait_recv()
    send_on("R", OWN, COLS)

    def load_columns():
        copies = [
            pltpu.make_async_copy(pc, pc_s, local_sem.at[0]),
            pltpu.make_async_copy(lc, lc_s, local_sem.at[1]),
        ]
        for copy in copies:
            copy.start()
        for copy in copies:
            copy.wait()

    def find_row(i, carry):
        js = [cs_ref[s, i] for s in range(KC)]
        js = [jnp.where(j >= 0, j, -2) for j in js]

        def find(n, inner):
            m = lc_s[n // KC, n % KC, i]
            there = jnp.maximum(m, 0)
            core, row = there // ROWS % 2, there % ROWS
            held = [pc_s[n // KC, core, u, row] for u in range(KC)]
            start = (core * ROWS + row) * 2
            spot = i * 32 + n
            for s in range(KC):
                hit = [v == js[s] for v in held]
                at = jnp.where(hit[0] | hit[1], start, jnp.where(hit[2] | hit[3], start + 1, ZERO))
                at_s[spot * KC + s] = jnp.where(m >= 0, at, ZERO)
                odd = hit[1] | hit[3]
                if s % 2 == 0:
                    low_s[spot * 2 + s // 2] = jnp.where(odd, 64, 0)
                else:
                    high_s[spot * 2 + s // 2] = jnp.where(odd, 128, 64)
            return inner

        return lax.fori_loop(0, 32, find, carry, unroll=4)

    def split(v):
        hi = v.astype(jnp.bfloat16)
        return hi, (v - hi.astype(jnp.float32)).astype(jnp.bfloat16)

    left_half = lane < 64

    def group_product(i, g, block):
        high, low = [], []
        for t in range(KC):
            spot = i * 32 + g * KC + t
            tiles = []
            for h in range(2):
                one = block(at_s[spot * KC + 2 * h])
                two = block(at_s[spot * KC + 2 * h + 1])
                kept = (lane >= low_s[spot * 2 + h]) & (lane < high_s[spot * 2 + h])
                straight = jnp.where(left_half, one, two)
                swapped = pltpu.roll(jnp.where(left_half, two, one), 64, 1)
                tiles.append(jnp.where(kept, straight, swapped))
            hi, lo = split(jnp.concatenate(tiles, axis=1))
            high.append(hi)
            low.append(lo)
        w_hi = jnp.concatenate(high, axis=0)
        w_lo = jnp.concatenate(low, axis=0)
        a_hi, a_lo = split(jnp.concatenate([lp[g, i, 0], lp[g, i, 1]], axis=1))
        first = jnp.dot(jnp.concatenate([a_hi, a_lo], axis=0), w_hi, preferred_element_type=jnp.float32)
        second = jnp.dot(a_hi, w_lo, preferred_element_type=jnp.float32)
        return first[:64] + first[64:] + second

    def store_slots(out_ref, i, read):
        for h in range(2):
            even = read(h, pl.ds(0, 32, stride=2))
            odd = read(h, pl.ds(1, 32, stride=2))
            out_ref[i, pl.ds(2 * h, 32, stride=4), :] = jnp.where(lane_half, even, pltpu.roll(odd, 64, 1))
            out_ref[i, pl.ds(2 * h + 1, 32, stride=4), :] = jnp.where(lane_half, pltpu.roll(even, 64, 1), odd)

    def square_piece(k, carry):
        def square_row(n, inner):
            i = k * STEP + n

            def add(g, total):
                return total + group_product(i, g, lambda at: rp[g * SPAN + at])

            total = lax.fori_loop(0, N_C, add, jnp.zeros((64, 256), jnp.float32), unroll=8)
            spot = place.core * CHUNK + 2 * i
            sp[0][spot] = total[:, :128]
            sp[0][spot + 1] = total[:, 128:]
            store_slots(sq_ref, i, lambda h, rows: sp[0][spot + h, rows, :])
            return inner

        lax.fori_loop(0, STEP, square_row, 0)
        for link, child in (("+", (1, 0)), ("-", (3, 0)), ("pair", (0, 1))):
            start_one("S", OWN, k, link, child, k)
        to_sibling("S", OWN, k)
        return carry

    def update_source(message, first, last):
        g = place.row_source(message) // 2
        panel = sp[slot(message)]

        def update_rows(n, carry):
            rows = [n * GROUP + i for i in range(GROUP)]
            totals = [group_product(i, g, lambda at: panel[at]) for i in rows]
            for i, total in zip(rows, totals):
                for h in range(2):
                    half = total[:, h * 128 : h * 128 + 128]
                    if not first:
                        half = half + acc[i, h]
                    if last:
                        half = 1.5 * rp[home + 2 * i + h] - 0.5 * half
                    acc[i, h] = half
                if last:
                    store_slots(up_ref, i, lambda h, rows: acc[i, h, rows, :])
            return carry

        lax.fori_loop(0, ROWS // GROUP, update_rows, 0)

    def follow(event):
        kind, name, message, piece = event
        if kind == "find":
            if piece == 0:
                load_columns()
            find_row(piece, 0)
        elif kind == "send":
            send_on(name, message, piece)
            if name == "R":
                to_sibling(name, message, piece)
        elif kind == "arrive":
            arrive(name, message, piece)
        elif kind == "use":
            from_sibling("S", message)
            update_source(message, not used, len(used) == 7)
            used.append(message)
        elif piece == 0:
            for m in MESSAGES:
                from_sibling("R", m)
            lax.fori_loop(0, TOGETHER, square_piece, 0)
        elif piece >= TOGETHER:
            square_piece(piece, 0)

    used = []
    events = whole_plan()
    while events:
        if events[0][0] == "square":
            limit = TOGETHER - 1 if events[0][3] == 0 else events[0][3]
            for event in [e for e in events if e[0] in ("find", "send") or e[1] == "L" and e[3] <= limit]:
                events.remove(event)
                follow(event)
        follow(events.pop(0))

    for name in ("R", "L", "S"):
        remote(rp.at[pl.ds(0, 7 * CHUNK)], send.at[number[name]], receive[name].at[0, 0], sibling).wait_send()
    for name in ("R", "S"):
        sem, n = sib_sems[name]
        remote(rp.at[pl.ds(0, 8 * CHUNK)], send.at[n], sem.at[0], sibling).wait_send()
    remote(pc.at[pl.ds(0, 7)], cols_send.at[0], r_recv.at[0, 0], sibling).wait_send()
    remote(lc.at[pl.ds(0, 7)], cols_send.at[1], l_recv.at[0, 0], sibling).wait_send()
    remote(mine, cols_send.at[3], pair_sem.at[0], sibling).wait_send()


def local(x_blocks, block_cols):
    x = x_blocks.reshape(ROWS, KC, 32, 128).transpose(0, 2, 1, 3).reshape(ROWS, 128, 128)
    cols = block_cols.T
    out = jax.ShapeDtypeStruct((ROWS, 128, 128), jnp.float32)
    vmem = pl.BlockSpec(memory_space=pltpu.VMEM)
    dma = pltpu.SemaphoreType.DMA
    square, updated = pl.pallas_call(
        kernel,
        out_shape=(out, out),
        in_specs=[vmem, vmem, pl.BlockSpec(memory_space=pltpu.SMEM)],
        out_specs=(vmem, vmem),
        scratch_shapes=[
            pltpu.VMEM((N_R // 2 * SPAN, 64, 128), jnp.float32),
            pltpu.VMEM((N_C, ROWS, 2, 64, 128), jnp.float32),
            pltpu.VMEM((ROWS, 2, 64, 128), jnp.float32),
            pltpu.VMEM((N_R // 2, 2, 8, 128), jnp.int32),
            pltpu.VMEM((N_C, 8, 128), jnp.int32),
            pltpu.SMEM((N_R // 2, 2, 8, 128), jnp.int32),
            pltpu.SMEM((N_C, 8, 128), jnp.int32),
            pltpu.SMEM((ROWS * 32 * KC,), jnp.int32),
            pltpu.SMEM((ROWS * 32 * 2,), jnp.int32),
            pltpu.SMEM((ROWS * 32 * 2,), jnp.int32),
            dma((5,)),
            dma((4,)),
            dma((PIECES + 1, 8)),
            dma((PIECES + 1, 8)),
            dma((PIECES + 1, 8)),
            dma((8,)),
            dma((8,)),
            dma((1,)),
            dma((2,)),
        ]
        + [pltpu.VMEM((SPAN, 64, 128), jnp.float32)] * 8,
        compiler_params=pltpu.CompilerParams(
            collective_id=0, has_side_effects=True, vmem_limit_bytes=56 << 20
        ),
        cost_estimate=pl.CostEstimate(flops=1 << 30, bytes_accessed=4 << 20, transcendentals=0),
    )(x, cols, cols)

    def back(y):
        return y.reshape(ROWS, 32, KC, 128).transpose(0, 2, 1, 3).reshape(ROWS, KC, 4096)

    return back(square), back(updated)


def solution(mesh):
    return jax.shard_map(
        local,
        mesh=mesh,
        in_specs=(P("row", "col", None), P("row", "col")),
        out_specs=(P("row", "col", None), P("row", "col", None)),
        check_vma=False,
    )
```

```python
import heapq

import jax
import jax.numpy as jnp
from jax import lax
from jax.experimental import pallas as pl
from jax.experimental.pallas import tpu as pltpu
from jax.sharding import PartitionSpec as P

MESH = pl.DeviceIdType.MESH

ROWS = 16
KC = 4
N_R = 16
N_C = 8
PIECES = 8
STEP = ROWS // PIECES
PIECE_US = 23.0 / PIECES
HOP_US = 3.5
FIND_US, FIND_GAP = 22.0, 2.0
SQUARE_US = 1.1
R_GAP, L_GAP = 3.0, 6.0
CHUNK = 2 * ROWS
SPAN = 2 * CHUNK + 1
ZERO = 2 * CHUNK
TOGETHER = 4
GROUP = 8
COLS = PIECES

OWN = (0, 0)
MESSAGES = [(d, p) for d in range(4) for p in range(2)]


def slot(message):
    return message[0] * 2 + message[1]


def tree(piece, pair_first):
    def route(message):
        d, p = message
        if d == 2:
            forward = (piece + (p if pair_first else 0)) % 2 == 0
            ring = ["+", "+"] if forward else ["-", "-"]
        else:
            ring = [[], ["+"], None, ["-"]][d]
        pair = ["pair"] * p
        return tuple(pair + ring if pair_first else ring + pair)

    by_route = {route(m): m for m in MESSAGES}
    children = {m: [] for m in MESSAGES}
    for m in MESSAGES:
        if m != OWN:
            r = route(m)
            children[by_route[r[:-1]]].append((r[-1], m))
    return children


def plan(gathers):
    free = {}
    order = []
    queue = []
    count = 0
    for name, trees, links, starts in gathers:
        for piece in [COLS] + list(range(PIECES)):
            count += 1
            heapq.heappush(queue, (starts[piece] if piece != COLS else 0.0, count, name, OWN, piece))
    table = {name: (trees, links) for name, trees, links, _ in gathers}
    while queue:
        now, _, name, message, piece = heapq.heappop(queue)
        order.append((now, name, message, piece))
        trees, links = table[name]
        for link, child in trees[piece][message]:
            wire = links[link]
            start = max(now, free.get(wire, 0.0))
            free[wire] = start + (0.05 if piece == COLS else PIECE_US)
            count += 1
            heapq.heappush(queue, (free[wire] + HOP_US, count, name, child, piece))
    return sorted(order, key=lambda e: e[0])


def trees_of(pair_first):
    return [tree(k, pair_first[k]) for k in range(PIECES)] + [tree(0, True)]


R_TREES = trees_of([k not in (2, 3) for k in range(PIECES)])
L_TREES = trees_of([True] * PIECES)
S_TREES = trees_of([k % 8 not in (2, 5, 7) for k in range(PIECES)])
R_LINKS = {"+": "x+", "-": "x-", "pair": "y"}
L_LINKS = {"+": "z+", "-": "z-", "pair": "y"}


def whole_plan():
    first = [
        ("R", R_TREES, R_LINKS, [R_GAP * k for k in range(PIECES)]),
        ("L", L_TREES, L_LINKS, [L_GAP * k for k in range(PIECES)]),
    ]
    steps = plan(first)
    ready = max(t for t, name, _, _ in steps if name == "R")
    starts, now = [], ready + 2.0
    for k in range(PIECES):
        now = max(now, max(t for t, name, _, n in steps if name == "L" and n <= k) + 0.5) + SQUARE_US
        starts.append(now)
    steps = plan(first + [("S", S_TREES, R_LINKS, starts)])
    known = max(t for t, name, _, n in steps if name != "S" and n == COLS)
    events = [(max(known, FIND_US) + FIND_GAP * n, "find", "", None, n) for n in range(ROWS)]
    done = {}
    for t, name, message, piece in steps:
        if name == "S" and piece == COLS or message == OWN and name != "S" and piece in (COLS, 0):
            continue
        if message != OWN:
            events.append((t, "arrive", name, message, piece))
            if name == "S":
                done[message] = max(t, done.get(message, 0.0))
        elif name == "S":
            events.append((t - SQUARE_US, "square", name, message, piece))
        else:
            events.append((t, "send", name, message, piece))
    events += [(t + 3.0, "use", "S", message, 0) for message, t in done.items()]
    events.append((starts[-1] + 0.1, "use", "S", OWN, 0))
    events.sort(key=lambda e: e[0])
    return [e[1:] for e in events]


class Place:
    def __init__(self):
        self.r = lax.axis_index("row")
        self.c = lax.axis_index("col")
        self.core = self.r % 2
        self.x = (self.r // 2) % 4
        self.yl = self.r // 8
        self.z = self.c // 2
        self.yh = self.c % 2
        self.q = self.r // 2

    def row_of(self, x, yl, core):
        return (yl * 4 + x) * 2 + core

    def row_source(self, message):
        d, p = message
        yl = 1 - self.yl if p else self.yl
        return self.row_of((self.x + 4 - d) % 4, yl, self.core)

    def col_source(self, message):
        d, p = message
        yh = 1 - self.yh if p else self.yh
        return ((self.z + 4 - d) % 4) * 2 + yh

    def row_neighbour(self, link):
        if link == "pair":
            return (self.row_of(self.x, 1 - self.yl, self.core), self.c)
        return (self.row_of((self.x + (1 if link == "+" else 3)) % 4, self.yl, self.core), self.c)

    def col_neighbour(self, link):
        if link == "pair":
            return (self.r, self.z * 2 + 1 - self.yh)
        return (self.r, ((self.z + (1 if link == "+" else 3)) % 4) * 2 + self.yh)

    def sibling(self):
        return (self.row_of(self.x, self.yl, 1 - self.core), self.c)


def remote(ref, send, recv, device, to=None):
    return pltpu.make_async_remote_copy(
        src_ref=ref,
        dst_ref=ref if to is None else to,
        send_sem=send,
        recv_sem=recv,
        device_id=device,
        device_id_type=MESH,
    )


def kernel(
    x_ref, cols_ref, cs_ref, sq_out, up_out,
    sq_ref, up_ref, rp, lp, acc, pc, lc, pc_s, lc_s, at_s, low_s, high_s,
    send, cols_send, r_recv, l_recv, s_recv, r_sib, s_sib, pair_sem, local_sem, out_sem,
    *sp,
):
    place = Place()
    r, c, q = place.r, place.c, place.q
    sibling = place.sibling()
    lane = lax.broadcasted_iota(jnp.int32, (64, 128), 1)
    lane_half = lax.broadcasted_iota(jnp.int32, (32, 128), 1) < 64
    home = q * SPAN + place.core * CHUNK

    barrier = pltpu.get_barrier_semaphore()
    neighbours = [place.row_neighbour(k) for k in ("+", "-", "pair")]
    neighbours += [place.col_neighbour(k) for k in ("+", "-", "pair")] + [sibling]
    for device in neighbours:
        pl.semaphore_signal(barrier, inc=1, device_id=device, device_id_type=MESH)

    def convert(i, carry):
        for h in range(2):
            pair = []
            for u in (2 * h, 2 * h + 1):
                v = x_ref[i, pl.ds(u, 32, stride=4), :]
                pair.append(jnp.where(cs_ref[u, i] >= 0, v, 0.0))
            even = jnp.where(lane_half, pair[0], pltpu.roll(pair[1], 64, 1))
            odd = jnp.where(lane_half, pltpu.roll(pair[0], 64, 1), pair[1])
            for n, part in enumerate((even, odd)):
                rp[home + 2 * i + h, pl.ds(n, 32, stride=2), :] = part
                lp[c, i, h, pl.ds(n, 32, stride=2), :] = part
        return carry

    lax.fori_loop(0, ROWS, convert, 0)
    for n in range(8):
        rp[n * SPAN + ZERO] = jnp.zeros((64, 128), jnp.float32)
        sp[n][ZERO] = jnp.zeros((64, 128), jnp.float32)
    for tile in (pc.at[q, place.core], lc.at[c]):
        tile[...] = jnp.zeros((8, 128), jnp.int32)
        tile[:KC, :ROWS] = cols_ref[...]
    pl.semaphore_wait(barrier, len(neighbours))

    def ref_of(name, message, piece, core=None):
        if name == "L":
            n = place.col_source(message)
            return lc.at[n] if piece == COLS else lp.at[n, pl.ds(piece * STEP, STEP)]
        first = (place.core if core is None else core) * CHUNK
        chip = place.row_source(message) // 2
        if name == "R" and piece == COLS:
            return pc.at[chip]
        n = CHUNK
        if piece is not None:
            first, n = first + piece * 2 * STEP, 2 * STEP
        if name == "S":
            return sp[slot(message)].at[pl.ds(first, n)]
        return rp.at[pl.ds(chip * SPAN + first, n)]

    trees = {"R": R_TREES, "L": L_TREES, "S": S_TREES}
    receive = {"R": r_recv, "L": l_recv, "S": s_recv}
    number = {"R": 0, "L": 1, "S": 2}

    def start_one(name, message, piece, link, child, index):
        device = place.col_neighbour(link) if name == "L" else place.row_neighbour(link)
        sem = cols_send.at[number[name]] if piece is COLS else send.at[number[name]]
        to = ref_of(name, child, piece) if name == "S" else None
        remote(ref_of(name, message, piece), sem, receive[name].at[index, slot(child)], device, to).start()

    def send_on(name, message, piece):
        for link, child in trees[name][piece][message]:
            start_one(name, message, piece, link, child, piece)

    def arrive(name, message, piece):
        remote(
            ref_of(name, message, piece), send.at[number[name]], receive[name].at[piece, slot(message)], sibling
        ).wait_recv()
        send_on(name, message, piece)
        if name != "L" and piece != COLS:
            to_sibling(name, message, piece)

    sib_sems = {"R": (r_sib, 3), "S": (s_sib, 4)}

    def to_sibling(name, message, piece):
        sem, n = sib_sems[name]
        remote(ref_of(name, message, piece), send.at[n], sem.at[slot(message)], sibling).start()

    def from_sibling(name, message):
        sem, n = sib_sems[name]
        whole = ref_of(name, message, None, 1 - place.core)
        remote(whole, send.at[n], sem.at[slot(message)], sibling).wait_recv()

    mine = pc.at[q, place.core]
    other = pc.at[q, 1 - place.core]
    remote(mine, cols_send.at[3], pair_sem.at[0], sibling).start()
    send_on("L", OWN, COLS)
    send_on("R", OWN, 0)
    send_on("L", OWN, 0)
    to_sibling("R", OWN, 0)
    remote(other, cols_send.at[3], pair_sem.at[0], sibling).wait_recv()
    send_on("R", OWN, COLS)

    def load_columns():
        copies = [
            pltpu.make_async_copy(pc, pc_s, local_sem.at[0]),
            pltpu.make_async_copy(lc, lc_s, local_sem.at[1]),
        ]
        for copy in copies:
            copy.start()
        for copy in copies:
            copy.wait()

    def find_row(i, carry):
        js = [cs_ref[s, i] for s in range(KC)]
        js = [jnp.where(j >= 0, j, -2) for j in js]

        def find(n, inner):
            m = lc_s[n // KC, n % KC, i]
            there = jnp.maximum(m, 0)
            core, row = there // ROWS % 2, there % ROWS
            held = [pc_s[n // KC, core, u, row] for u in range(KC)]
            start = (core * ROWS + row) * 2
            spot = i * 32 + n
            for s in range(KC):
                hit = [v == js[s] for v in held]
                at = jnp.where(hit[0] | hit[1], start, jnp.where(hit[2] | hit[3], start + 1, ZERO))
                at_s[spot * KC + s] = jnp.where(m >= 0, at, ZERO)
                odd = hit[1] | hit[3]
                if s % 2 == 0:
                    low_s[spot * 2 + s // 2] = jnp.where(odd, 64, 0)
                else:
                    high_s[spot * 2 + s // 2] = jnp.where(odd, 128, 64)
            return inner

        return lax.fori_loop(0, 32, find, carry, unroll=4)

    def split(v):
        hi = v.astype(jnp.bfloat16)
        return hi, (v - hi.astype(jnp.float32)).astype(jnp.bfloat16)

    left_half = lane < 64

    def group_product(i, g, block):
        high, low = [], []
        for t in range(KC):
            spot = i * 32 + g * KC + t
            tiles = []
            for h in range(2):
                one = block(at_s[spot * KC + 2 * h])
                two = block(at_s[spot * KC + 2 * h + 1])
                kept = (lane >= low_s[spot * 2 + h]) & (lane < high_s[spot * 2 + h])
                straight = jnp.where(left_half, one, two)
                swapped = pltpu.roll(jnp.where(left_half, two, one), 64, 1)
                tiles.append(jnp.where(kept, straight, swapped))
            hi, lo = split(jnp.concatenate(tiles, axis=1))
            high.append(hi)
            low.append(lo)
        w_hi = jnp.concatenate(high, axis=0)
        w_lo = jnp.concatenate(low, axis=0)
        a_hi, a_lo = split(jnp.concatenate([lp[g, i, 0], lp[g, i, 1]], axis=1))
        first = jnp.dot(jnp.concatenate([a_hi, a_lo], axis=0), w_hi, preferred_element_type=jnp.float32)
        second = jnp.dot(a_hi, w_lo, preferred_element_type=jnp.float32)
        return first[:64] + first[64:] + second

    def store_slots(out_ref, i, read):
        for h in range(2):
            even = read(h, pl.ds(0, 32, stride=2))
            odd = read(h, pl.ds(1, 32, stride=2))
            out_ref[i, pl.ds(2 * h, 32, stride=4), :] = jnp.where(lane_half, even, pltpu.roll(odd, 64, 1))
            out_ref[i, pl.ds(2 * h + 1, 32, stride=4), :] = jnp.where(lane_half, pltpu.roll(even, 64, 1), odd)

    def square_piece(k, carry):
        def square_row(n, inner):
            i = k * STEP + n

            def add(g, total):
                return total + group_product(i, g, lambda at: rp[g * SPAN + at])

            total = lax.fori_loop(0, N_C, add, jnp.zeros((64, 256), jnp.float32), unroll=8)
            spot = place.core * CHUNK + 2 * i
            sp[0][spot] = total[:, :128]
            sp[0][spot + 1] = total[:, 128:]
            store_slots(sq_ref, i, lambda h, rows: sp[0][spot + h, rows, :])
            return inner

        lax.fori_loop(0, STEP, square_row, 0)
        for link, child in (("+", (1, 0)), ("-", (3, 0)), ("pair", (0, 1))):
            start_one("S", OWN, k, link, child, k)
        to_sibling("S", OWN, k)
        return carry

    def update_source(message, first, last):
        g = place.row_source(message) // 2
        panel = sp[slot(message)]

        def update_rows(n, carry):
            rows = [n * GROUP + i for i in range(GROUP)]
            totals = [group_product(i, g, lambda at: panel[at]) for i in rows]
            for i, total in zip(rows, totals):
                for h in range(2):
                    half = total[:, h * 128 : h * 128 + 128]
                    if not first:
                        half = half + acc[i, h]
                    if last:
                        half = 1.5 * rp[home + 2 * i + h] - 0.5 * half
                    acc[i, h] = half
                if last:
                    store_slots(up_ref, i, lambda h, rows: acc[i, h, rows, :])
            return carry

        if last:
            for n in range(ROWS // GROUP):
                update_rows(n, 0)
                write_out(n + 1).start()
        else:
            lax.fori_loop(0, ROWS // GROUP, update_rows, 0)

    def follow(event):
        kind, name, message, piece = event
        if kind == "find":
            if piece == 0:
                load_columns()
            find_row(piece, 0)
        elif kind == "send":
            send_on(name, message, piece)
            if name == "R":
                to_sibling(name, message, piece)
        elif kind == "arrive":
            arrive(name, message, piece)
        elif kind == "use":
            from_sibling("S", message)
            update_source(message, not used, len(used) == 7)
            used.append(message)
        elif piece == 0:
            for m in MESSAGES:
                from_sibling("R", m)
            lax.fori_loop(0, TOGETHER, square_piece, 0)
        elif piece >= TOGETHER:
            square_piece(piece, 0)
            if piece == PIECES - 1:
                write_out(0).start()

    def write_out(n):
        if n == 0:
            return pltpu.make_async_copy(sq_ref, sq_out, out_sem.at[0])
        rows = pl.ds((n - 1) * GROUP, GROUP)
        return pltpu.make_async_copy(up_ref.at[rows], up_out.at[rows], out_sem.at[n])

    used = []
    events = whole_plan()
    while events:
        if events[0][0] == "square":
            limit = TOGETHER - 1 if events[0][3] == 0 else events[0][3]
            for event in [e for e in events if e[0] in ("find", "send") or e[1] == "L" and e[3] <= limit]:
                events.remove(event)
                follow(event)
        follow(events.pop(0))

    for n in range(ROWS // GROUP + 1):
        write_out(n).wait()
    for name in ("R", "L", "S"):
        remote(rp.at[pl.ds(0, 7 * CHUNK)], send.at[number[name]], receive[name].at[0, 0], sibling).wait_send()
    for name in ("R", "S"):
        sem, n = sib_sems[name]
        remote(rp.at[pl.ds(0, 8 * CHUNK)], send.at[n], sem.at[0], sibling).wait_send()
    remote(pc.at[pl.ds(0, 7)], cols_send.at[0], r_recv.at[0, 0], sibling).wait_send()
    remote(lc.at[pl.ds(0, 7)], cols_send.at[1], l_recv.at[0, 0], sibling).wait_send()
    remote(mine, cols_send.at[3], pair_sem.at[0], sibling).wait_send()


def local(x_blocks, block_cols):
    x = x_blocks.reshape(ROWS, KC, 32, 128).transpose(0, 2, 1, 3).reshape(ROWS, 128, 128)
    cols = block_cols.T
    out = jax.ShapeDtypeStruct((ROWS, 128, 128), jnp.float32)
    vmem = pl.BlockSpec(memory_space=pltpu.VMEM)
    dma = pltpu.SemaphoreType.DMA
    square, updated = pl.pallas_call(
        kernel,
        out_shape=(out, out),
        in_specs=[vmem, vmem, pl.BlockSpec(memory_space=pltpu.SMEM)],
        out_specs=(pl.BlockSpec(memory_space=pl.ANY),) * 2,
        scratch_shapes=[
            pltpu.VMEM((ROWS, 128, 128), jnp.float32),
            pltpu.VMEM((ROWS, 128, 128), jnp.float32),
            pltpu.VMEM((N_R // 2 * SPAN, 64, 128), jnp.float32),
            pltpu.VMEM((N_C, ROWS, 2, 64, 128), jnp.float32),
            pltpu.VMEM((ROWS, 2, 64, 128), jnp.float32),
            pltpu.VMEM((N_R // 2, 2, 8, 128), jnp.int32),
            pltpu.VMEM((N_C, 8, 128), jnp.int32),
            pltpu.SMEM((N_R // 2, 2, 8, 128), jnp.int32),
            pltpu.SMEM((N_C, 8, 128), jnp.int32),
            pltpu.SMEM((ROWS * 32 * KC,), jnp.int32),
            pltpu.SMEM((ROWS * 32 * 2,), jnp.int32),
            pltpu.SMEM((ROWS * 32 * 2,), jnp.int32),
            dma((5,)),
            dma((4,)),
            dma((PIECES + 1, 8)),
            dma((PIECES + 1, 8)),
            dma((PIECES + 1, 8)),
            dma((8,)),
            dma((8,)),
            dma((1,)),
            dma((2,)),
            dma((ROWS // GROUP + 1,)),
        ]
        + [pltpu.VMEM((SPAN, 64, 128), jnp.float32)] * 8,
        compiler_params=pltpu.CompilerParams(
            collective_id=0, has_side_effects=True, vmem_limit_bytes=56 << 20
        ),
        cost_estimate=pl.CostEstimate(flops=1 << 30, bytes_accessed=4 << 20, transcendentals=0),
    )(x, cols, cols)

    def back(y):
        return y.reshape(ROWS, 32, KC, 128).transpose(0, 2, 1, 3).reshape(ROWS, KC, 4096)

    return back(square), back(updated)


def solution(mesh):
    return jax.shard_map(
        local,
        mesh=mesh,
        in_specs=(P("row", "col", None), P("row", "col")),
        out_specs=(P("row", "col", None), P("row", "col", None)),
        check_vma=False,
    )
```
